1024 devices in a mesh: dp: 4 (over x), expert: 16 (over y, z_hi), tensor: 16 (over z_lo, core).
Axes of the slice: x: 4, y: 4, z: 32 (z_hi: 4, z_lo: 8; z = z_hi * 8 + z_lo), core: 2. Of those that a mesh axis runs over, the one named last changes fastest.
Arguments:
- grad_out: bfloat16 [2048, 6144], P(('dp', 'expert', 'tensor')), may hold values from -6 to 6
- route_ids: int32 [2048, 4], P(('dp', 'expert', 'tensor')), may hold values from 0 to 15, all different within a row; in each aligned block of 32 rows (0 to 31, 32 to 63, ...) at most 10 rows name the same one
- route_probs: bfloat16 [2048, 4], P(('dp', 'expert', 'tensor')), may hold values from 0.099609375 to 1
- gate_up: bfloat16 [4, 16, 16, 10, 2, 5376], P('dp', 'expert', None, None, None, 'tensor'), may hold values from -5 to 5
- w_down: bfloat16 [16, 5376, 6144], P('expert', 'tensor'), may hold values from -0.078125 to 0.078125
Outputs:
- grad_pre: bfloat16 [4, 16, 16, 10, 2, 5376], P('dp', 'expert', None, None, None, 'tensor')
- grad_w_down: bfloat16 [16, 5376, 6144], P('expert', 'tensor', 'dp')
The draws below stay inside these ranges and needn't reach their ends.
Inputs may be any that keep to these rules, and one draw needn't show every extreme that they name: `route_ids`: in each aligned block of 32 tokens no expert is named by more than 10 of them; a token names distinct experts.
All inputs are finite; a program needn't handle non-finite values.
Results may differ from the reference program's by a relative error of at most 0.013.
Values may be sent and summed in bfloat16 or wider, within the bound.
A program may use at most 32 MiB of HBM per device.

```python
import math
import jax
import jax.numpy as jnp
import numpy as np
from jax import lax

D = 6144
FF = 5376
TOP = 4
TOK_DEV = 2
EXPERTS = 16
CAP = 10
TOKENS = 2048
N_DP = 4
N_EXPERT = 16
N_TENSOR = 16


def levels(stream_key, dims, split, low, largest):
    loudness, own = 1.0, jax.random.fold_in(stream_key, 6)
    for axis_at, blocks in split:
        draws = jnp.exp(jax.random.uniform(jax.random.fold_in(own, axis_at), (blocks,), jnp.float32, low / len(split), largest / len(split)))
        loudness = loudness * jnp.repeat(draws, dims[axis_at] // blocks).reshape([-1 if axis == axis_at else 1 for axis in range(len(dims))])
    return loudness


def shared_out(own_key, own, number, rows, count, top, limit, lean):
    sequence = jax.random.permutation(own_key, count)
    crowded, usual = portions_of(count, rows * top, limit, lean, True), portions_of(count, rows * top, limit, lean, False)
    places = jnp.arange(count)

    def named(lengths, rotation):
        used = int((lengths > 0).sum())
        fixed = max(1, used // 4)
        moved = fixed + (places - fixed + rotation * (used - fixed)) % max(1, count - fixed)
        return jnp.zeros((count,), jnp.int32).at[sequence[jnp.where(places < fixed, places, moved)]].set(jnp.asarray(lengths, jnp.int32))

    lengths = jnp.where(number % 4 == 0, named(crowded, number // 4), named(usual, number - number // 4 - 1))
    mixed = jax.random.permutation(jax.random.fold_in(own, 3), count)
    source_of, receiver = mixed[0:count // 2 * 2:2], mixed[1:count // 2 * 2:2]
    room = jnp.minimum(lengths[source_of] - 1, limit - lengths[receiver]) // 2
    room = jnp.where((source_of == sequence[0]) | (receiver == sequence[0]) | (lengths[receiver] == 0), 0, jnp.maximum(room, 0))
    moved = jax.random.randint(jax.random.fold_in(own, 4), (count // 2,), 0, 1 << 20) % (room + 1)
    lengths = lengths.at[source_of].add(-moved).at[receiver].add(moved)
    members = jnp.searchsorted(jnp.cumsum(lengths), jnp.arange(rows * top), side="right").astype(jnp.int32)
    table = members.reshape(top, rows).T
    table = table[jax.random.permutation(jax.random.fold_in(own, 1), rows)]
    rotation = jax.random.randint(jax.random.fold_in(own, 2), (rows, 1), 0, top)
    return jnp.take_along_axis(table, (jnp.arange(top)[None, :] + rotation) % top, axis=1)


def portions_of(amount, total, bound, lean, full):
    weights = [(1 << 20) // math.isqrt(standing ** lean) + 1 for standing in range(1, amount + 1)]
    largest = bound if full else min(bound, max(-(-total // amount), total * weights[0] // sum(weights)))
    least = 1 if total - largest >= amount - 1 else 0
    counts, rest = [largest] + [least] * (amount - 1), total - largest - least * (amount - 1)
    while rest > 0:
        free = [i for i in range(1, amount) if counts[i] < largest] or [i for i in range(1, amount) if counts[i] < bound]
        whole, remaining = sum([weights[i] for i in free]), rest
        for i in free:
            more = min(bound - counts[i], max(1, remaining * weights[i] // whole), rest)
            counts[i] = counts[i] + more
            rest = rest - more
    return np.array(counts)


def bell_draw(own_key, dims, scale, bound, cuts=(), kind=jnp.bfloat16):
    drawn = scale * jax.random.normal(own_key, dims, jnp.float32)
    if cuts:
        drawn = drawn * levels(own_key, dims, cuts, -0.22, 0.18)
    return jnp.clip(drawn, -bound, bound).astype(kind)


def setup_inputs(seed: int = 0) -> dict:
    seeds = jax.random.split(jax.random.key(seed), 6)
    grad_out = bell_draw(seeds[0], (TOKENS, D), 1.0, 6.0, ((0, 1024),))
    route_ids_keys = jax.random.split(jax.random.fold_in(seeds[1], 1), TOKENS // (TOK_DEV * N_TENSOR))
    route_ids_turns = jax.random.permutation(jax.random.fold_in(seeds[1], 3), TOKENS // (TOK_DEV * N_TENSOR))
    route_ids = jax.vmap(lambda own, number: shared_out(jax.random.fold_in(seeds[1], 2), own, number, TOK_DEV * N_TENSOR, EXPERTS, TOP, CAP, 2))(route_ids_keys, route_ids_turns).reshape((TOKENS, TOP))
    route_probs = jnp.clip(jnp.exp(math.log(1.0) - 2.306499 * jax.random.uniform(seeds[2], (TOKENS, TOP), jnp.float32) ** levels(seeds[2], (TOKENS, TOP), ((0, 1024),), -0.2, 0.2)), 0.099609375, 1.0).astype(jnp.bfloat16)
    gate_up = bell_draw(seeds[3], (N_DP, EXPERTS, N_EXPERT, CAP, 2, FF), 1.0, 5.0, ((0, 4), (1, 16), (5, 16)))
    w_down = bell_draw(seeds[4], (EXPERTS, FF, D), FF ** -0.5, 0.078125, ((0, 16), (1, 16)))
    return dict(grad_out=grad_out, route_ids=route_ids, route_probs=route_probs, gate_up=gate_up, w_down=w_down)


def reference(grad_out, route_ids, route_probs, gate_up, w_down):
    groups = N_DP * N_EXPERT
    block = TOK_DEV * N_TENSOR
    width = block * TOP
    cot = grad_out.reshape(groups, block, D).astype(jnp.float32)
    ids = route_ids.reshape(groups, width)
    probs = route_probs.reshape(groups, width).astype(jnp.float32)
    rows = (probs[:, :, None] * jnp.repeat(cot, TOP, axis=1)).astype(jnp.bfloat16)
    onehot = (ids[:, :, None] == jnp.arange(EXPERTS, dtype=jnp.int32)[None, None, :]).astype(jnp.int32)
    place = jnp.sum((jnp.cumsum(onehot, axis=1) - 1) * onehot, axis=2)
    slot = ids * CAP + place
    select = (slot[:, None, :] == jnp.arange(EXPERTS * CAP, dtype=jnp.int32)[None, :, None]).astype(jnp.float32)
    routed = jnp.einsum('gsj,gjd->gsd', select, rows.astype(jnp.float32)).astype(jnp.bfloat16)
    routed = routed.reshape(N_DP, N_EXPERT, EXPERTS, CAP, D)
    routed = jnp.moveaxis(routed, 2, 1)

    def per_expert(index):
        received = routed[:, index].reshape(N_DP, N_EXPERT * CAP, D)
        weight = w_down[index]
        flat = received.reshape(N_DP * N_EXPERT * CAP, D)
        grad_hidden = lax.dot_general(flat, weight, (((1,), (1,)), ((), ())), preferred_element_type=jnp.float32)
        saved = gate_up[:, index].astype(jnp.float32).reshape(N_DP * N_EXPERT * CAP, 2, FF)
        gate = saved[:, 0]
        upper = saved[:, 1]
        sig = jax.nn.sigmoid(gate)
        d_gate = grad_hidden * upper * sig * (1.0 + gate * (1.0 - sig))
        d_upper = grad_hidden * gate * sig
        grad_pre = jnp.stack([d_gate, d_upper], axis=1).astype(jnp.bfloat16).reshape(N_DP, N_EXPERT, CAP, 2, FF)
        hidden = (gate * sig * upper).astype(jnp.bfloat16).reshape(N_DP, N_EXPERT * CAP, FF)
        total = jnp.zeros((FF, D), jnp.float32)
        for replica in range(N_DP):
            part = lax.dot_general(hidden[replica], received[replica], (((0,), (0,)), ((), ())), preferred_element_type=jnp.float32).astype(jnp.bfloat16)
            part = lax.optimization_barrier(part)
            total = total + part.astype(jnp.float32)
        return grad_pre, total.astype(jnp.bfloat16)

    grad_pre, grad_w = lax.map(per_expert, jnp.arange(EXPERTS, dtype=jnp.int32))
    return jnp.moveaxis(grad_pre, 0, 1), grad_w
```

```python
import jax
import jax.numpy as jnp
from jax import lax
from jax.experimental import pallas as pl
from jax.experimental.pallas import tpu as pltpu
from jax.sharding import PartitionSpec as P

F32 = jnp.float32
BF16 = jnp.bfloat16
HALF = 768
META = 128
WIDE = HALF + META
SUB = 40
PAD = 48
CHUNK = 160
NT = (((1,), (1,)), ((), ()))


def kernel(ext, gate, up, w_hbm, dgate, dup, gw, stage, tok, ypack, relay, rows, wv, before,
           hid, hid_t, coef_g, coef_u, rs_out, rs_in, w_sem, x_sem, h_sem, a_sem, cw_sem, ccw_sem,
           yr_sem, yd_sem, yf_sem, d_sem, r_sem):
    x, e, t = lax.axis_index("dp"), lax.axis_index("expert"), lax.axis_index("tensor")
    y, zhi = e // 4, e % 4
    zlo, c = t // 2, t % 2
    z = zhi * 8 + zlo
    width = gate.shape[2]

    def at(x_to, y_to, z_to, c_to):
        return (x_to, y_to * 4 + z_to // 8, (z_to % 8) * 2 + c_to)

    def send(src, dst, sems, index, to):
        copy = pltpu.make_async_remote_copy(
            src_ref=src, dst_ref=dst, send_sem=sems.at[(0,) + index], recv_sem=sems.at[(1,) + index],
            device_id=to, device_id_type=pl.DeviceIdType.MESH)
        copy.start()
        return copy

    load_w = pltpu.make_async_copy(
        w_hbm.at[0, :, pl.ds(pl.multiple_of(x * (2 * HALF), 128), 2 * HALF)], wv, w_sem)
    load_w.start()

    next_y, last_y, far_y = (y + 1) % 4, (y + 3) % 4, (y + 2) % 4
    next_z, last_z = (z + 1) % 32, (z + 31) % 32
    sibling = at(x, y, z, 1 - c)
    partners = [at((x + dx) % 4, y, z, (c + dc) % 2) for dx in range(4) for dc in range(2) if dx or dc]
    partners += [at(x, y, (z + 8 * dz) % 32, c) for dz in (1, 2, 3)]
    partners += [at(x, y, next_z, c), at(x, y, last_z, c), at(x, next_y, z, c), at(x, last_y, z, c)]
    barrier = pltpu.get_barrier_semaphore()
    for device in partners:
        pl.semaphore_signal(barrier, inc=1, device_id=device, device_id_type=pl.DeviceIdType.MESH)
    pl.semaphore_wait(barrier, len(partners))

    x_copies = []
    for dx in range(4):
        for dc in range(2):
            if dx or dc:
                xd, cd = (x + dx) % 4, (c + dc) % 2
                x_copies.append(send(ext.at[xd * 2 + cd], stage.at[x * 2 + c], x_sem, (dx * 2 + dc,),
                                     at(xd, y, z, cd)))
    stage[x * 2 + c] = ext[x * 2 + c]

    for part in range(4):
        g, u = gate[part].astype(F32), up[part].astype(F32)
        s = jax.nn.sigmoid(g)
        coef_g[part] = u * s * (1.0 + g * (1.0 - s))
        coef_u[part] = g * s
        hid[x, part, 0:SUB] = (g * s * u).astype(BF16)
        hid[x, part, SUB:PAD] = jnp.zeros((PAD - SUB, width), BF16)
    h_copies = [send(hid.at[x], hid.at[x], h_sem, (dx,), at((x + dx) % 4, y, z, c)) for dx in (1, 2, 3)]

    for copy in x_copies:
        copy.wait_recv()
    tok[zlo, zhi] = stage[...].reshape(16, WIDE)
    a_copies = [send(tok.at[zlo, zhi], tok.at[zlo, zhi], a_sem, (dz,), at(x, y, (z + 8 * dz) % 32, c))
                for dz in (1, 2, 3)]

    from_row = lax.broadcasted_iota(jnp.int32, (512, 512), 0)
    to_row = lax.broadcasted_iota(jnp.int32, (512, 512), 1)
    same = ((from_row >> 2) & 15) == ((to_row >> 2) & 15)
    before[...] = jnp.where(same & (from_row < to_row), 1.0, 0.0).astype(BF16)

    for copy in a_copies:
        copy.wait_recv()

    b_copies = []
    cw, ccw = None, None
    for step in range(4):
        b_next, b_last = (zlo + 8 - step) % 8, (zlo + step) % 8
        if step < 3:
            src_next, src_last = tok.at[b_next], tok.at[b_last]
        else:
            src_next, src_last = tok.at[b_next, pl.ds(0, 2)], tok.at[b_last, pl.ds(2, 2)]
        if cw is not None:
            cw.wait_recv()
        cw = send(src_next, src_next, cw_sem, (step,), at(x, y, next_z, c))
        if ccw is not None:
            ccw.wait_recv()
        ccw = send(src_last, src_last, ccw_sem, (step,), at(x, y, last_z, c))
        b_copies += [cw, ccw]
    cw.wait_recv()
    ccw.wait_recv()

    meta = tok[:, :, :, HALF:WIDE].reshape(512, META)
    pick = (lax.broadcasted_iota(jnp.int32, (8, META), 0) ==
            lax.broadcasted_iota(jnp.int32, (8, META), 1)).astype(F32).astype(BF16)
    meta_t = lax.dot_general(pick, meta, NT, preferred_element_type=F32)
    step_y = lax.broadcasted_iota(jnp.int32, (8, 512), 0)
    expert = (((step_y + y) & 3) * 4 + zhi).astype(F32)
    named = jnp.zeros((8, 512), F32)
    prob = jnp.zeros((8, 512), F32)
    for k in range(4):
        hit = meta_t[k:k + 1, :] == expert
        named = named + jnp.where(hit, 1.0, 0.0)
        prob = prob + jnp.where(hit, meta_t[4 + k:5 + k, :], 0.0)
    place = jnp.dot(named.astype(BF16), before[...], preferred_element_type=F32)
    token = lax.broadcasted_iota(jnp.int32, (8, 512), 1)
    base = (((token >> 2) & 3) * SUB + ((token >> 4) & 3) * 10).astype(F32)
    slot = jnp.where(named > 0.5, base + place, -1.0)
    slots = lax.broadcasted_iota(jnp.int32, (CHUNK, 512), 0).astype(F32)

    def packed(d):
        select = jnp.where(slots == slot[d:d + 1, :], prob[d:d + 1, :], 0.0).astype(BF16)
        data = tok[:, :, :, 0:HALF].reshape(512, HALF)
        return jnp.dot(select, data, preferred_element_type=F32).astype(BF16)

    first, second = pl.ds(0, CHUNK // 2), pl.ds(CHUNK // 2, CHUNK // 2)
    to_next, to_last = at(x, next_y, z, c), at(x, last_y, z, c)
    ypack[2] = packed(2)
    yr_next = send(ypack.at[2, first], relay.at[0], yr_sem, (0,), to_next)
    yr_last = send(ypack.at[2, second], relay.at[1], yr_sem, (1,), to_last)
    ypack[0] = packed(1)
    yd_next = send(ypack.at[0], rows.at[c, y], yd_sem, (0,), to_next)
    ypack[1] = packed(3)
    yd_last = send(ypack.at[1], rows.at[c, y], yd_sem, (1,), to_last)
    rows[c, y] = packed(0)
    d_copies = [send(rows.at[c, y], rows.at[c, y], d_sem, (0,), sibling)]

    for copy in h_copies:
        copy.wait_recv()
    load_w.wait()
    for part in range(4):
        chunk = jnp.concatenate([hid[r, part].astype(F32)[0:SUB] for r in range(4)], axis=0)
        hid_t[part * CHUNK:(part + 1) * CHUNK] = chunk.astype(BF16)

    yr_next.wait_recv()
    yf_next = send(relay.at[0], rows.at[c, last_y, first], yf_sem, (0,), to_next)
    yr_last.wait_recv()
    yf_last = send(relay.at[1], rows.at[c, next_y, second], yf_sem, (1,), to_last)

    r_copies = []

    def partial(i, part):
        d_copies[i].wait_recv()
        gh = lax.dot_general(rows[0, part], wv[:, 0:HALF], NT, preferred_element_type=F32)
        gh = gh + lax.dot_general(rows[1, part], wv[:, HALF:2 * HALF], NT, preferred_element_type=F32)
        for r in range(4):
            rs_out[part, r, 0:SUB] = gh[r * SUB:(r + 1) * SUB].astype(BF16)
            rs_out[part, r, SUB:PAD] = jnp.zeros((PAD - SUB, width), BF16)
        r_copies.append([send(rs_out.at[part, (x + dx) % 4], rs_in.at[x, part], r_sem, (i, dx),
                              at((x + dx) % 4, y, z, c)) for dx in (1, 2, 3)])

    partial(0, y)
    yd_next.wait_recv()
    d_copies.append(send(rows.at[c, last_y], rows.at[c, last_y], d_sem, (1,), sibling))
    yd_last.wait_recv()
    d_copies.append(send(rows.at[c, next_y], rows.at[c, next_y], d_sem, (2,), sibling))
    partial(1, last_y)
    partial(2, next_y)
    yf_next.wait_recv()
    yf_last.wait_recv()
    d_copies.append(send(rows.at[c, far_y], rows.at[c, far_y], d_sem, (3,), sibling))
    partial(3, far_y)

    for core in range(2):
        gw[:, core * HALF:(core + 1) * HALF] = lax.dot_general(
            hid_t[...], rows[core].reshape(4 * CHUNK, HALF), (((0,), (0,)), ((), ())),
            preferred_element_type=F32).astype(BF16)

    for i, part in enumerate((y, last_y, next_y, far_y)):
        for copy in r_copies[i]:
            copy.wait_recv()
        gh = rs_out[part, x].astype(F32)[0:SUB]
        for dx in (1, 2, 3):
            gh = gh + rs_in[(x + dx) % 4, part].astype(F32)[0:SUB]
        dgate[part] = (gh * coef_g[part]).astype(BF16)
        dup[part] = (gh * coef_u[part]).astype(BF16)

    sent = x_copies + h_copies + a_copies + b_copies + d_copies
    sent += [yr_next, yr_last, yd_next, yd_last, yf_next, yf_last]
    for group in r_copies:
        sent += group
    for copy in sent:
        copy.wait_send()


def per_device(grad_out, route_ids, route_probs, gate_up, w_down):
    width = gate_up.shape[5]
    meta = jnp.concatenate([route_ids.astype(BF16), route_probs, jnp.zeros((2, META - 8), BF16)], axis=1)
    cot = jnp.moveaxis(grad_out.reshape(2, 8, HALF), 1, 0)
    ext = jnp.concatenate([cot, jnp.broadcast_to(meta[None], (8, 2, META))], axis=2)
    saved = gate_up.reshape(4, SUB, 2, width)
    vmem = pl.BlockSpec(memory_space=pltpu.VMEM)
    dma = pltpu.SemaphoreType.DMA
    dgate, dup, gw = pl.pallas_call(
        kernel,
        out_shape=(
            jax.ShapeDtypeStruct((4, SUB, width), BF16),
            jax.ShapeDtypeStruct((4, SUB, width), BF16),
            jax.ShapeDtypeStruct((width, 2 * HALF), BF16),
        ),
        in_specs=[vmem, vmem, vmem, pl.BlockSpec(memory_space=pl.ANY)],
        out_specs=(vmem, vmem, vmem),
        scratch_shapes=[
            pltpu.VMEM((8, 2, WIDE), BF16),
            pltpu.VMEM((8, 4, 16, WIDE), BF16),
            pltpu.VMEM((3, CHUNK, HALF), BF16),
            pltpu.VMEM((2, CHUNK // 2, HALF), BF16),
            pltpu.VMEM((2, 4, CHUNK, HALF), BF16),
            pltpu.VMEM((width, 2 * HALF), BF16),
            pltpu.VMEM((512, 512), BF16),
            pltpu.VMEM((4, 4, PAD, width), BF16),
            pltpu.VMEM((4 * CHUNK, width), BF16),
            pltpu.VMEM((4, SUB, width), F32),
            pltpu.VMEM((4, SUB, width), F32),
            pltpu.VMEM((4, 4, PAD, width), BF16),
            pltpu.VMEM((4, 4, PAD, width), BF16),
            dma(()),
            dma((2, 8)),
            dma((2, 4)),
            dma((2, 4)),
            dma((2, 4)),
            dma((2, 4)),
            dma((2, 2)),
            dma((2, 2)),
            dma((2, 2)),
            dma((2, 4)),
            dma((2, 4, 4)),
        ],
        compiler_params=pltpu.CompilerParams(
            collective_id=0, has_side_effects=True, vmem_limit_bytes=48 * 1024 * 1024
        ),
    )(ext, saved[:, :, 0], saved[:, :, 1], w_down)
    grad_pre = jnp.stack([dgate, dup], axis=2).reshape(gate_up.shape)
    return grad_pre, gw[None]


def solution(mesh):
    return jax.shard_map(
        per_device,
        mesh=mesh,
        in_specs=(
            P(("dp", "expert", "tensor"), None),
            P(("dp", "expert", "tensor"), None),
            P(("dp", "expert", "tensor"), None),
            P("dp", "expert", None, None, None, "tensor"),
            P("expert", "tensor", None),
        ),
        out_specs=(P("dp", "expert", None, None, None, "tensor"), P("expert", "tensor", "dp")),
        check_vma=False,
    )
```

```python
import jax
import jax.numpy as jnp
from jax import lax
from jax.experimental import pallas as pl
from jax.experimental.pallas import tpu as pltpu
from jax.sharding import PartitionSpec as P

F32 = jnp.float32
BF16 = jnp.bfloat16
HALF = 768
META = 128
PART = HALF // 2
FIRST = META + PART
WIDE = HALF + META
SUB = 40
PAD = 48
CHUNK = 160
NT = (((1,), (1,)), ((), ()))


def kernel(cot, ids, probs, saved, w_hbm, dgate, dup, gw, ext, stage, tok_a, tok_b, ypack, rows, wv, before,
           hid, hid_t, coef_g, coef_u, g_sum, rs_out, rs_in, w_sem, x_sem, h_sem, a_sem, b_sem, y_sem, d_sem,
           r_sem):
    x, e, t = lax.axis_index("dp"), lax.axis_index("expert"), lax.axis_index("tensor")
    y, zhi = e // 4, e % 4
    zlo, c = t // 2, t % 2
    z = zhi * 8 + zlo
    width = saved.shape[3]

    def at(x_to, y_to, z_to, c_to):
        return (x_to, y_to * 4 + z_to // 8, (z_to % 8) * 2 + c_to)

    def send(src, dst, sems, index, to):
        copy = pltpu.make_async_remote_copy(
            src_ref=src, dst_ref=dst, send_sem=sems.at[(0,) + index], recv_sem=sems.at[(1,) + index],
            device_id=to, device_id_type=pl.DeviceIdType.MESH)
        copy.start()
        return copy

    load_w = pltpu.make_async_copy(
        w_hbm.at[0, :, pl.ds(pl.multiple_of(x * (2 * HALF), 128), 2 * HALF)], wv, w_sem)
    load_w.start()

    next_y, last_y, far_y = (y + 1) % 4, (y + 3) % 4, (y + 2) % 4
    sibling = at(x, y, z, 1 - c)
    partners = [at((x + dx) % 4, y, z, (c + dc) % 2) for dx in range(4) for dc in range(2) if dx or dc]
    partners += [at(x, y, (z + 8 * dz) % 32, c) for dz in (1, 2, 3)]
    partners += [at(x, y, (z + dz) % 32, c) for dz in (1, 31, 2, 30)]
    partners += [at(x, y_to, z, c) for y_to in (next_y, last_y, far_y)]
    barrier = pltpu.get_barrier_semaphore()
    for device in partners:
        pl.semaphore_signal(barrier, inc=1, device_id=device, device_id_type=pl.DeviceIdType.MESH)

    lane = lax.broadcasted_iota(jnp.int32, (2, META), 1)
    meta = jnp.zeros((2, META), F32)
    for k in range(4):
        meta = jnp.where(lane == k, ids[:, k:k + 1].astype(F32), meta)
        meta = jnp.where(lane == 4 + k, probs[:, k:k + 1].astype(F32), meta)
    for q in range(8):
        ext[q, :, META:WIDE] = cot[:, q * HALF:(q + 1) * HALF]
        ext[q, :, 0:META] = meta.astype(BF16)
    pl.semaphore_wait(barrier, len(partners))

    x_copies = []
    for dx in range(4):
        for dc in range(2):
            if dx or dc:
                xd, cd = (x + dx) % 4, (c + dc) % 2
                x_copies.append(send(ext.at[xd * 2 + cd], stage.at[x * 2 + c], x_sem, (dx * 2 + dc,),
                                     at(xd, y, z, cd)))
    stage[x * 2 + c] = ext[x * 2 + c]

    for copy in x_copies:
        copy.wait_recv()
    toks = (tok_a, tok_b)
    tok_a[zlo, zhi] = stage[:, :, 0:FIRST].reshape(16, FIRST)
    tok_b[zlo, zhi] = stage[:, :, FIRST:WIDE].reshape(16, PART)

    a_copies, b_copies = {}, {}
    for h in range(2):
        for k in (2, 1, 3):
            own = toks[h].at[zlo, zhi]
            a_copies[h, k] = send(own, own, a_sem, (h * 4 + k,), at(x, y, (z + 32 - 8 * k) % 32, c))

    def pass_on(h, way, k, held, far):
        origin = (z + 32 - way * held) % 32
        block = toks[h].at[origin % 8, (origin // 8 + k) % 4]
        index = h * 32 + (way + 1) // 2 * 16 + k * 4 + held + far - 1
        b_copies[h, way, k, held + far] = send(block, block, b_sem, (index,),
                                               at(x, y, (z + 32 + way * far) % 32, c))

    def spread(h, k):
        if k:
            a_copies[h, k].wait_recv()
        for way in (1, -1):
            pass_on(h, way, k, 0, 2)
            pass_on(h, way, k, 0, 1)

    def spread_on(h, k):
        for way in (1, -1):
            b_copies[h, way, k, 2].wait_recv()
            pass_on(h, way, k, 2, 1)
            if k in (0, 3 if way == 1 else 1):
                pass_on(h, way, k, 2, 2)

    def gathered(h):
        for way in (1, -1):
            for k in range(4):
                b_copies[h, way, k, 1].wait_recv()
                b_copies[h, way, k, 3].wait_recv()
            for k in (0, 3 if way == 1 else 1):
                b_copies[h, way, k, 4].wait_recv()

    for h in range(2):
        spread(h, 0)

    for part in range(4):
        both = saved[part].astype(F32)
        g, u = both[:, 0, :], both[:, 1, :]
        s = jax.nn.sigmoid(g)
        coef_g[part] = u * s * (1.0 + g * (1.0 - s))
        coef_u[part] = g * s
        hid[x, part, 0:SUB] = (g * s * u).astype(BF16)
        hid[x, part, SUB:PAD] = jnp.zeros((PAD - SUB, width), BF16)
    h_copies = [send(hid.at[x], hid.at[x], h_sem, (dx,), at((x + dx) % 4, y, z, c)) for dx in (1, 2, 3)]

    from_row = lax.broadcasted_iota(jnp.int32, (512, 512), 0)
    to_row = lax.broadcasted_iota(jnp.int32, (512, 512), 1)
    same = ((from_row >> 2) & 15) == ((to_row >> 2) & 15)
    before[...] = jnp.where(same & (from_row < to_row), 1.0, 0.0).astype(BF16)
    for h in range(2):
        for k in (1, 3, 2):
            spread(h, k)
    for h in range(2):
        for k in (0, 1, 3, 2):
            spread_on(h, k)
    gathered(0)

    meta = tok_a[:, :, :, 0:META].reshape(512, META)
    pick = (lax.broadcasted_iota(jnp.int32, (8, META), 0) ==
            lax.broadcasted_iota(jnp.int32, (8, META), 1)).astype(F32).astype(BF16)
    meta_t = lax.dot_general(pick, meta, NT, preferred_element_type=F32)
    step_y = lax.broadcasted_iota(jnp.int32, (8, 512), 0)
    expert = (((step_y + y) & 3) * 4 + zhi).astype(F32)
    named = jnp.zeros((8, 512), F32)
    prob = jnp.zeros((8, 512), F32)
    for k in range(4):
        hit = meta_t[k:k + 1, :] == expert
        named = named + jnp.where(hit, 1.0, 0.0)
        prob = prob + jnp.where(hit, meta_t[4 + k:5 + k, :], 0.0)
    place = jnp.dot(named.astype(BF16), before[...], preferred_element_type=F32)
    token = lax.broadcasted_iota(jnp.int32, (8, 512), 1)
    base = (((token >> 2) & 3) * SUB + ((token >> 4) & 3) * 10).astype(F32)
    slot = jnp.where(named > 0.5, base + place, -1.0)
    slots = lax.broadcasted_iota(jnp.int32, (CHUNK, 512), 0).astype(F32)

    y_copies, d_copies = {}, {}

    def pack(h):
        data = (tok_a[:, :, :, META:FIRST] if h == 0 else tok_b[...]).reshape(512, PART)
        for d in (2, 1, 3, 0):
            select = jnp.where(slots == slot[d:d + 1, :], prob[d:d + 1, :], 0.0).astype(BF16)
            packed = jnp.dot(select, data, preferred_element_type=F32).astype(BF16)
            own = rows.at[h, c, y]
            if d:
                ypack[h, d - 1] = packed
                y_copies[h, d] = send(ypack.at[h, d - 1], own, y_sem, (h * 4 + d,), at(x, (y + d) % 4, z, c))
            else:
                rows[h, c, y] = packed
                d_copies[h, 0] = send(own, own, d_sem, (h * 4,), sibling)

    pack(0)
    gathered(1)
    pack(1)

    for copy in h_copies:
        copy.wait_recv()
    load_w.wait()
    for part in range(4):
        chunk = jnp.concatenate([hid[r, part].astype(F32)[0:SUB] for r in range(4)], axis=0)
        hid_t[part * CHUNK:(part + 1) * CHUNK] = chunk.astype(BF16)

    chunks = (y, last_y, next_y, far_y)
    r_copies = []

    def share(h):
        for i, d in ((1, 1), (2, 3), (3, 2)):
            y_copies[h, d].wait_recv()
            block = rows.at[h, c, chunks[i]]
            d_copies[h, i] = send(block, block, d_sem, (h * 4 + i,), sibling)

    def product(h, i):
        d_copies[h, i].wait_recv()
        low = h * PART
        return (lax.dot_general(rows[h, 0, chunks[i]], wv[:, low:low + PART], NT, preferred_element_type=F32) +
                lax.dot_general(rows[h, 1, chunks[i]], wv[:, HALF + low:HALF + low + PART], NT,
                                preferred_element_type=F32))

    share(0)
    for i in range(4):
        g_sum[i] = product(0, i)
    share(1)
    for i, part in enumerate(chunks):
        gh = product(1, i) + g_sum[i]
        for r in range(4):
            rs_out[part, r, 0:SUB] = gh[r * SUB:(r + 1) * SUB].astype(BF16)
            rs_out[part, r, SUB:PAD] = jnp.zeros((PAD - SUB, width), BF16)
        r_copies.append([send(rs_out.at[part, (x + dx) % 4], rs_in.at[x, part], r_sem, (i, dx),
                              at((x + dx) % 4, y, z, c)) for dx in (1, 2, 3)])

    for core in range(2):
        for h in range(2):
            low = core * HALF + h * PART
            gw[:, low:low + PART] = lax.dot_general(
                hid_t[...], rows[h, core].reshape(4 * CHUNK, PART), (((0,), (0,)), ((), ())),
                preferred_element_type=F32).astype(BF16)

    for i, part in enumerate(chunks):
        for copy in r_copies[i]:
            copy.wait_recv()
        gh = rs_out[part, x].astype(F32)[0:SUB]
        for dx in (1, 2, 3):
            gh = gh + rs_in[(x + dx) % 4, part].astype(F32)[0:SUB]
        dgate[part] = (gh * coef_g[part]).astype(BF16)
        dup[part] = (gh * coef_u[part]).astype(BF16)

    sent = x_copies + h_copies
    for group in (a_copies, b_copies, y_copies, d_copies):
        sent += group.values()
    for group in r_copies:
        sent += group
    for copy in sent:
        copy.wait_send()


def per_device(grad_out, route_ids, route_probs, gate_up, w_down):
    width = gate_up.shape[5]
    vmem = pl.BlockSpec(memory_space=pltpu.VMEM)
    dma = pltpu.SemaphoreType.DMA
    dgate, dup, gw = pl.pallas_call(
        kernel,
        out_shape=(
            jax.ShapeDtypeStruct((4, SUB, width), BF16),
            jax.ShapeDtypeStruct((4, SUB, width), BF16),
            jax.ShapeDtypeStruct((width, 2 * HALF), BF16),
        ),
        in_specs=[vmem, vmem, vmem, vmem, pl.BlockSpec(memory_space=pl.ANY)],
        out_specs=(vmem, vmem, vmem),
        scratch_shapes=[
            pltpu.VMEM((8, 2, WIDE), BF16),
            pltpu.VMEM((8, 2, WIDE), BF16),
            pltpu.VMEM((8, 4, 16, FIRST), BF16),
            pltpu.VMEM((8, 4, 16, PART), BF16),
            pltpu.VMEM((2, 3, CHUNK, PART), BF16),
            pltpu.VMEM((2, 2, 4, CHUNK, PART), BF16),
            pltpu.VMEM((width, 2 * HALF), BF16),
            pltpu.VMEM((512, 512), BF16),
            pltpu.VMEM((4, 4, PAD, width), BF16),
            pltpu.VMEM((4 * CHUNK, width), BF16),
            pltpu.VMEM((4, SUB, width), F32),
            pltpu.VMEM((4, SUB, width), F32),
            pltpu.VMEM((4, CHUNK, width), F32),
            pltpu.VMEM((4, 4, PAD, width), BF16),
            pltpu.VMEM((4, 4, PAD, width), BF16),
            dma(()),
            dma((2, 8)),
            dma((2, 4)),
            dma((2, 8)),
            dma((2, 64)),
            dma((2, 8)),
            dma((2, 8)),
            dma((2, 4, 4)),
        ],
        compiler_params=pltpu.CompilerParams(
            collective_id=0, has_side_effects=True, vmem_limit_bytes=60 * 1024 * 1024
        ),
    )(grad_out, route_ids, route_probs, gate_up.reshape(4, SUB, 2, width), w_down)
    grad_pre = jnp.stack([dgate, dup], axis=2).reshape(gate_up.shape)
    return grad_pre, gw[None]


def solution(mesh):
    return jax.shard_map(
        per_device,
        mesh=mesh,
        in_specs=(
            P(("dp", "expert", "tensor"), None),
            P(("dp", "expert", "tensor"), None),
            P(("dp", "expert", "tensor"), None),
            P("dp", "expert", None, None, None, "tensor"),
            P("expert", "tensor", None),
        ),
        out_specs=(P("dp", "expert", None, None, None, "tensor"), P("expert", "tensor", "dp")),
        check_vma=False,
    )
```

```python
import jax
import jax.numpy as jnp
from jax import lax
from jax.experimental import pallas as pl
from jax.experimental.pallas import tpu as pltpu
from jax.sharding import PartitionSpec as P

F32 = jnp.float32
BF16 = jnp.bfloat16
HALF = 768
META = 128
PART = HALF // 2
FIRST = META + PART
WIDE = HALF + META
SUB = 40
PAD = 48
CHUNK = 160
NT = (((1,), (1,)), ((), ()))


def kernel(cot, ids, probs, saved, w_hbm, dpre, gw, ext, stage, tok_a, tok_b, ypack, rows, wv, before,
           hid, hid_t, coef_g, coef_u, g_sum, rs_out, rs_in, w_sem, x_sem, h_sem, a_sem, b_sem, y_sem, d_sem,
           r_sem):
    x, e, t = lax.axis_index("dp"), lax.axis_index("expert"), lax.axis_index("tensor")
    y, zhi = e // 4, e % 4
    zlo, c = t // 2, t % 2
    z = zhi * 8 + zlo
    width = saved.shape[3]

    def at(x_to, y_to, z_to, c_to):
        return (x_to, y_to * 4 + z_to // 8, (z_to % 8) * 2 + c_to)

    def send(src, dst, sems, index, to):
        copy = pltpu.make_async_remote_copy(
            src_ref=src, dst_ref=dst, send_sem=sems.at[(0,) + index], recv_sem=sems.at[(1,) + index],
            device_id=to, device_id_type=pl.DeviceIdType.MESH)
        copy.start()
        return copy

    load_w = pltpu.make_async_copy(
        w_hbm.at[0, :, pl.ds(pl.multiple_of(x * (2 * HALF), 128), 2 * HALF)], wv, w_sem)
    load_w.start()

    next_y, last_y, far_y = (y + 1) % 4, (y + 3) % 4, (y + 2) % 4
    sibling = at(x, y, z, 1 - c)
    partners = [at((x + dx) % 4, y, z, (c + dc) % 2) for dx in range(4) for dc in range(2) if dx or dc]
    partners += [at(x, y, (z + 8 * dz) % 32, c) for dz in (1, 2, 3)]
    partners += [at(x, y, (z + dz) % 32, c) for dz in (1, 31, 2, 30)]
    partners += [at(x, y_to, z, c) for y_to in (next_y, last_y, far_y)]
    barrier = pltpu.get_barrier_semaphore()
    for device in partners:
        pl.semaphore_signal(barrier, inc=1, device_id=device, device_id_type=pl.DeviceIdType.MESH)

    lane = lax.broadcasted_iota(jnp.int32, (2, META), 1)
    meta = jnp.zeros((2, META), F32)
    for k in range(4):
        meta = jnp.where(lane == k, ids[:, k:k + 1].astype(F32), meta)
        meta = jnp.where(lane == 4 + k, probs[:, k:k + 1].astype(F32), meta)
    for q in range(8):
        ext[q, :, META:WIDE] = cot[:, q * HALF:(q + 1) * HALF]
        ext[q, :, 0:META] = meta.astype(BF16)
    pl.semaphore_wait(barrier, len(partners))

    x_copies = []
    for dx in range(4):
        for dc in range(2):
            if dx or dc:
                xd, cd = (x + dx) % 4, (c + dc) % 2
                x_copies.append(send(ext.at[xd * 2 + cd], stage.at[x * 2 + c], x_sem, (dx * 2 + dc,),
                                     at(xd, y, z, cd)))
    stage[x * 2 + c] = ext[x * 2 + c]

    for copy in x_copies:
        copy.wait_recv()
    toks = (tok_a, tok_b)
    tok_a[zlo, zhi] = stage[:, :, 0:FIRST].reshape(16, FIRST)
    tok_b[zlo, zhi] = stage[:, :, FIRST:WIDE].reshape(16, PART)

    a_copies, b_copies = {}, {}
    for h in range(2):
        for k in (2, 1, 3):
            own = toks[h].at[zlo, zhi]
            a_copies[h, k] = send(own, own, a_sem, (h * 4 + k,), at(x, y, (z + 32 - 8 * k) % 32, c))

    def pass_on(h, way, k, held, far):
        origin = (z + 32 - way * held) % 32
        block = toks[h].at[origin % 8, (origin // 8 + k) % 4]
        index = h * 32 + (way + 1) // 2 * 16 + k * 4 + held + far - 1
        b_copies[h, way, k, held + far] = send(block, block, b_sem, (index,),
                                               at(x, y, (z + 32 + way * far) % 32, c))

    def spread(h, k):
        if k:
            a_copies[h, k].wait_recv()
        for way in (1, -1):
            pass_on(h, way, k, 0, 2)
            pass_on(h, way, k, 0, 1)

    def spread_on(h, k):
        for way in (1, -1):
            b_copies[h, way, k, 2].wait_recv()
            pass_on(h, way, k, 2, 1)
            if k in (0, 3 if way == 1 else 1):
                pass_on(h, way, k, 2, 2)

    def gathered(h):
        for way in (1, -1):
            for k in range(4):
                b_copies[h, way, k, 1].wait_recv()
                b_copies[h, way, k, 3].wait_recv()
            for k in (0, 3 if way == 1 else 1):
                b_copies[h, way, k, 4].wait_recv()

    for h in range(2):
        spread(h, 0)

    for part in range(4):
        both = saved[part].astype(F32)
        g, u = both[:, 0, :], both[:, 1, :]
        s = jax.nn.sigmoid(g)
        coef_g[part] = u * s * (1.0 + g * (1.0 - s))
        coef_u[part] = g * s
        hid[x, part, 0:SUB] = (g * s * u).astype(BF16)
        hid[x, part, SUB:PAD] = jnp.zeros((PAD - SUB, width), BF16)
    h_copies = [send(hid.at[x], hid.at[x], h_sem, (dx,), at((x + dx) % 4, y, z, c)) for dx in (1, 2, 3)]

    from_row = lax.broadcasted_iota(jnp.int32, (512, 512), 0)
    to_row = lax.broadcasted_iota(jnp.int32, (512, 512), 1)
    same = ((from_row >> 2) & 15) == ((to_row >> 2) & 15)
    before[...] = jnp.where(same & (from_row < to_row), 1.0, 0.0).astype(BF16)
    for h in range(2):
        for k in (1, 3, 2):
            spread(h, k)
    for h in range(2):
        for k in (0, 1, 3, 2):
            spread_on(h, k)
    gathered(0)

    meta = tok_a[:, :, :, 0:META].reshape(512, META)
    pick = (lax.broadcasted_iota(jnp.int32, (8, META), 0) ==
            lax.broadcasted_iota(jnp.int32, (8, META), 1)).astype(F32).astype(BF16)
    meta_t = lax.dot_general(pick, meta, NT, preferred_element_type=F32)
    step_y = lax.broadcasted_iota(jnp.int32, (8, 512), 0)
    expert = (((step_y + y) & 3) * 4 + zhi).astype(F32)
    named = jnp.zeros((8, 512), F32)
    prob = jnp.zeros((8, 512), F32)
    for k in range(4):
        hit = meta_t[k:k + 1, :] == expert
        named = named + jnp.where(hit, 1.0, 0.0)
        prob = prob + jnp.where(hit, meta_t[4 + k:5 + k, :], 0.0)
    place = jnp.dot(named.astype(BF16), before[...], preferred_element_type=F32)
    token = lax.broadcasted_iota(jnp.int32, (8, 512), 1)
    base = (((token >> 2) & 3) * SUB + ((token >> 4) & 3) * 10).astype(F32)
    slot = jnp.where(named > 0.5, base + place, -1.0)
    slots = lax.broadcasted_iota(jnp.int32, (CHUNK, 512), 0).astype(F32)

    y_copies, d_copies = {}, {}

    def pack(h):
        data = (tok_a[:, :, :, META:FIRST] if h == 0 else tok_b[...]).reshape(512, PART)
        for d in (2, 1, 3, 0):
            select = jnp.where(slots == slot[d:d + 1, :], prob[d:d + 1, :], 0.0).astype(BF16)
            packed = jnp.dot(select, data, preferred_element_type=F32).astype(BF16)
            own = rows.at[h, c, y]
            if d:
                ypack[h, d - 1] = packed
                y_copies[h, d] = send(ypack.at[h, d - 1], own, y_sem, (h * 4 + d,), at(x, (y + d) % 4, z, c))
            else:
                rows[h, c, y] = packed
                d_copies[h, 0] = send(own, own, d_sem, (h * 4,), sibling)

    pack(0)
    gathered(1)
    pack(1)

    for copy in h_copies:
        copy.wait_recv()
    load_w.wait()
    for part in range(4):
        chunk = jnp.concatenate([hid[r, part].astype(F32)[0:SUB] for r in range(4)], axis=0)
        hid_t[part * CHUNK:(part + 1) * CHUNK] = chunk.astype(BF16)

    chunks = (y, last_y, next_y, far_y)
    r_copies = []

    def share(h):
        for i, d in ((1, 1), (2, 3), (3, 2)):
            y_copies[h, d].wait_recv()
            block = rows.at[h, c, chunks[i]]
            d_copies[h, i] = send(block, block, d_sem, (h * 4 + i,), sibling)

    def product(h, i):
        d_copies[h, i].wait_recv()
        low = h * PART
        return (lax.dot_general(rows[h, 0, chunks[i]], wv[:, low:low + PART], NT, preferred_element_type=F32) +
                lax.dot_general(rows[h, 1, chunks[i]], wv[:, HALF + low:HALF + low + PART], NT,
                                preferred_element_type=F32))

    share(0)
    for i in range(4):
        g_sum[i] = product(0, i)
    share(1)
    for i, part in enumerate(chunks):
        gh = product(1, i) + g_sum[i]
        for r in range(4):
            rs_out[part, r, 0:SUB] = gh[r * SUB:(r + 1) * SUB].astype(BF16)
            rs_out[part, r, SUB:PAD] = jnp.zeros((PAD - SUB, width), BF16)
        r_copies.append([send(rs_out.at[part, (x + dx) % 4], rs_in.at[x, part], r_sem, (i, dx),
                              at((x + dx) % 4, y, z, c)) for dx in (1, 2, 3)])

    for core in range(2):
        for h in range(2):
            low = core * HALF + h * PART
            gw[:, low:low + PART] = lax.dot_general(
                hid_t[...], rows[h, core].reshape(4 * CHUNK, PART), (((0,), (0,)), ((), ())),
                preferred_element_type=F32).astype(BF16)

    for i, part in enumerate(chunks):
        for copy in r_copies[i]:
            copy.wait_recv()
        gh = rs_out[part, x].astype(F32)[0:SUB]
        for dx in (1, 2, 3):
            gh = gh + rs_in[(x + dx) % 4, part].astype(F32)[0:SUB]
        dpre[0, part] = (gh * coef_g[part]).astype(BF16)
        dpre[1, part] = (gh * coef_u[part]).astype(BF16)

    sent = x_copies + h_copies
    for group in (a_copies, b_copies, y_copies, d_copies):
        sent += group.values()
    for group in r_copies:
        sent += group
    for copy in sent:
        copy.wait_send()


def per_device(grad_out, route_ids, route_probs, gate_up, w_down):
    width = gate_up.shape[5]
    vmem = pl.BlockSpec(memory_space=pltpu.VMEM)
    dma = pltpu.SemaphoreType.DMA
    dpre, gw = pl.pallas_call(
        kernel,
        out_shape=(
            jax.ShapeDtypeStruct((2, 4, SUB, width), BF16),
            jax.ShapeDtypeStruct((width, 2 * HALF), BF16),
        ),
        in_specs=[vmem, vmem, vmem, vmem, pl.BlockSpec(memory_space=pl.ANY)],
        out_specs=(vmem, vmem),
        scratch_shapes=[
            pltpu.VMEM((8, 2, WIDE), BF16),
            pltpu.VMEM((8, 2, WIDE), BF16),
            pltpu.VMEM((8, 4, 16, FIRST), BF16),
            pltpu.VMEM((8, 4, 16, PART), BF16),
            pltpu.VMEM((2, 3, CHUNK, PART), BF16),
            pltpu.VMEM((2, 2, 4, CHUNK, PART), BF16),
            pltpu.VMEM((width, 2 * HALF), BF16),
            pltpu.VMEM((512, 512), BF16),
            pltpu.VMEM((4, 4, PAD, width), BF16),
            pltpu.VMEM((4 * CHUNK, width), BF16),
            pltpu.VMEM((4, SUB, width), F32),
            pltpu.VMEM((4, SUB, width), F32),
            pltpu.VMEM((4, CHUNK, width), F32),
            pltpu.VMEM((4, 4, PAD, width), BF16),
            pltpu.VMEM((4, 4, PAD, width), BF16),
            dma(()),
            dma((2, 8)),
            dma((2, 4)),
            dma((2, 8)),
            dma((2, 64)),
            dma((2, 8)),
            dma((2, 8)),
            dma((2, 4, 4)),
        ],
        compiler_params=pltpu.CompilerParams(
            collective_id=0, has_side_effects=True, vmem_limit_bytes=60 * 1024 * 1024
        ),
    )(grad_out, route_ids, route_probs, gate_up.reshape(4, SUB, 2, width), w_down)
    grad_pre = jnp.moveaxis(dpre, 0, 2).reshape(gate_up.shape)
    return grad_pre, gw[None]


def solution(mesh):
    return jax.shard_map(
        per_device,
        mesh=mesh,
        in_specs=(
            P(("dp", "expert", "tensor"), None),
            P(("dp", "expert", "tensor"), None),
            P(("dp", "expert", "tensor"), None),
            P("dp", "expert", None, None, None, "tensor"),
            P("expert", "tensor", None),
        ),
        out_specs=(P("dp", "expert", None, None, None, "tensor"), P("expert", "tensor", "dp")),
        check_vma=False,
    )
```

```python
import jax
import jax.numpy as jnp
from jax import lax
from jax.experimental import pallas as pl
from jax.experimental.pallas import tpu as pltpu
from jax.sharding import PartitionSpec as P

F32 = jnp.float32
BF16 = jnp.bfloat16
HALF = 768
META = 128
PART = HALF // 2
FIRST = META + PART
WIDE = HALF + META
SUB = 40
PAD = 48
CHUNK = 160
NT = (((1,), (1,)), ((), ()))


def kernel(cot, ids, probs, saved, w_hbm, dpre, gw, ext, stage, tok_a, tok_b, ypack, rows, wv, before,
           hid, hid_t, coef_g, coef_u, g_sum, rs_out, rs_in, w_sem, x_sem, h_sem, a_sem, b_sem, y_sem, d_sem,
           r_sem):
    x, e, t = lax.axis_index("dp"), lax.axis_index("expert"), lax.axis_index("tensor")
    y, zhi = e // 4, e % 4
    zlo, c = t // 2, t % 2
    z = zhi * 8 + zlo
    width = saved.shape[3]

    def at(x_to, y_to, z_to, c_to):
        return (x_to, y_to * 4 + z_to // 8, (z_to % 8) * 2 + c_to)

    def send(src, dst, sems, index, to):
        copy = pltpu.make_async_remote_copy(
            src_ref=src, dst_ref=dst, send_sem=sems.at[(0,) + index], recv_sem=sems.at[(1,) + index],
            device_id=to, device_id_type=pl.DeviceIdType.MESH)
        copy.start()
        return copy

    load_w = pltpu.make_async_copy(
        w_hbm.at[0, :, pl.ds(pl.multiple_of(x * (2 * HALF), 128), 2 * HALF)], wv, w_sem)
    load_w.start()

    next_y, last_y, far_y = (y + 1) % 4, (y + 3) % 4, (y + 2) % 4
    sibling = at(x, y, z, 1 - c)
    partners = [at((x + dx) % 4, y, z, (c + dc) % 2) for dx in range(4) for dc in range(2) if dx or dc]
    partners += [at(x, y, (z + 8 * dz) % 32, c) for dz in (1, 2, 3)]
    partners += [at(x, y, (z + dz) % 32, c) for dz in (1, 31, 2, 30)]
    partners += [at(x, y_to, z, c) for y_to in (next_y, last_y, far_y)]
    barrier = pltpu.get_barrier_semaphore()
    for device in partners:
        pl.semaphore_signal(barrier, inc=1, device_id=device, device_id_type=pl.DeviceIdType.MESH)

    lane = lax.broadcasted_iota(jnp.int32, (2, META), 1)
    meta = jnp.zeros((2, META), F32)
    for k in range(4):
        meta = jnp.where(lane == k, ids[:, k:k + 1].astype(F32), meta)
        meta = jnp.where(lane == 4 + k, probs[:, k:k + 1].astype(F32), meta)
    for q in range(8):
        ext[q, :, META:WIDE] = cot[:, q * HALF:(q + 1) * HALF]
        ext[q, :, 0:META] = meta.astype(BF16)
    pl.semaphore_wait(barrier, len(partners))

    x_copies = []
    for dx in range(4):
        for dc in range(2):
            if dx or dc:
                xd, cd = (x + dx) % 4, (c + dc) % 2
                x_copies.append(send(ext.at[xd * 2 + cd], stage.at[x * 2 + c], x_sem, (dx * 2 + dc,),
                                     at(xd, y, z, cd)))
    stage[x * 2 + c] = ext[x * 2 + c]

    for copy in x_copies:
        copy.wait_recv()
    toks = (tok_a, tok_b)
    tok_a[zlo, zhi] = stage[:, :, 0:FIRST].reshape(16, FIRST)
    tok_b[zlo, zhi] = stage[:, :, FIRST:WIDE].reshape(16, PART)

    a_copies, b_copies = {}, {}
    for h in range(2):
        for k in (2, 1, 3):
            own = toks[h].at[zlo, zhi]
            a_copies[h, k] = send(own, own, a_sem, (h * 4 + k,), at(x, y, (z + 32 - 8 * k) % 32, c))

    def pass_on(h, way, k, held, far):
        origin = (z + 32 - way * held) % 32
        block = toks[h].at[origin % 8, (origin // 8 + k) % 4]
        index = h * 32 + (way + 1) // 2 * 16 + k * 4 + held + far - 1
        b_copies[h, way, k, held + far] = send(block, block, b_sem, (index,),
                                               at(x, y, (z + 32 + way * far) % 32, c))

    def spread(h, k):
        if k:
            a_copies[h, k].wait_recv()
        for way in (1, -1):
            pass_on(h, way, k, 0, 2)
            pass_on(h, way, k, 0, 1)

    def spread_on(h, k):
        for way in (1, -1):
            b_copies[h, way, k, 2].wait_recv()
            pass_on(h, way, k, 2, 1)
            if k in (0, 3 if way == 1 else 1):
                pass_on(h, way, k, 2, 2)

    def gathered(h):
        for way in (1, -1):
            for k in range(4):
                b_copies[h, way, k, 1].wait_recv()
                b_copies[h, way, k, 3].wait_recv()
            for k in (0, 3 if way == 1 else 1):
                b_copies[h, way, k, 4].wait_recv()

    for h in range(2):
        spread(h, 0)

    for part in range(4):
        both = saved[part].astype(F32)
        g, u = both[:, 0, :], both[:, 1, :]
        s = jax.nn.sigmoid(g)
        coef_g[part] = u * s * (1.0 + g * (1.0 - s))
        coef_u[part] = g * s
        hid[x, part, 0:SUB] = (g * s * u).astype(BF16)
        hid[x, part, SUB:PAD] = jnp.zeros((PAD - SUB, width), BF16)
    h_copies = [send(hid.at[x], hid.at[x], h_sem, (dx,), at((x + dx) % 4, y, z, c)) for dx in (1, 2, 3)]

    from_row = lax.broadcasted_iota(jnp.int32, (512, 512), 0)
    to_row = lax.broadcasted_iota(jnp.int32, (512, 512), 1)
    same = ((from_row >> 2) & 15) == ((to_row >> 2) & 15)
    before[...] = jnp.where(same & (from_row < to_row), 1.0, 0.0).astype(BF16)
    for h in range(2):
        for k in (1, 3, 2):
            spread(h, k)
    for h in range(2):
        for k in (0, 1, 3, 2):
            spread_on(h, k)
    gathered(0)

    meta = tok_a[:, :, :, 0:META].reshape(512, META)
    pick = (lax.broadcasted_iota(jnp.int32, (8, META), 0) ==
            lax.broadcasted_iota(jnp.int32, (8, META), 1)).astype(F32).astype(BF16)
    meta_t = lax.dot_general(pick, meta, NT, preferred_element_type=F32)
    step_y = lax.broadcasted_iota(jnp.int32, (8, 512), 0)
    expert = (((step_y + y) & 3) * 4 + zhi).astype(F32)
    named = jnp.zeros((8, 512), F32)
    prob = jnp.zeros((8, 512), F32)
    for k in range(4):
        hit = meta_t[k:k + 1, :] == expert
        named = named + jnp.where(hit, 1.0, 0.0)
        prob = prob + jnp.where(hit, meta_t[4 + k:5 + k, :], 0.0)
    place = jnp.dot(named.astype(BF16), before[...], preferred_element_type=F32)
    token = lax.broadcasted_iota(jnp.int32, (8, 512), 1)
    base = (((token >> 2) & 3) * SUB + ((token >> 4) & 3) * 10).astype(F32)
    slot = jnp.where(named > 0.5, base + place, -1.0)
    slots = lax.broadcasted_iota(jnp.int32, (CHUNK, 512), 0).astype(F32)

    y_copies, d_copies = {}, {}

    def pack(h):
        data = (tok_a[:, :, :, META:FIRST] if h == 0 else tok_b[...]).reshape(512, PART)
        for d in (2, 1, 3, 0):
            select = jnp.where(slots == slot[d:d + 1, :], prob[d:d + 1, :], 0.0).astype(BF16)
            packed = jnp.dot(select, data, preferred_element_type=F32).astype(BF16)
            own = rows.at[h, c, y]
            if d:
                ypack[h, d - 1] = packed
                y_copies[h, d] = send(ypack.at[h, d - 1], own, y_sem, (h * 4 + d,), at(x, (y + d) % 4, z, c))
            else:
                rows[h, c, y] = packed
                d_copies[h, 0] = send(own, own, d_sem, (h * 4,), sibling)

    pack(0)
    gathered(1)
    pack(1)

    for copy in h_copies:
        copy.wait_recv()
    load_w.wait()
    for part in range(4):
        chunk = jnp.concatenate([hid[r, part].astype(F32)[0:SUB] for r in range(4)], axis=0)
        hid_t[part * CHUNK:(part + 1) * CHUNK] = chunk.astype(BF16)

    chunks = (y, last_y, next_y, far_y)
    r_copies = []

    def share(h):
        for i, d in ((1, 1), (2, 3), (3, 2)):
            y_copies[h, d].wait_recv()
            block = rows.at[h, c, chunks[i]]
            d_copies[h, i] = send(block, block, d_sem, (h * 4 + i,), sibling)

    def product(h, i):
        d_copies[h, i].wait_recv()
        low = h * PART
        return (lax.dot_general(rows[h, 0, chunks[i]], wv[:, low:low + PART], NT, preferred_element_type=F32) +
                lax.dot_general(rows[h, 1, chunks[i]], wv[:, HALF + low:HALF + low + PART], NT,
                                preferred_element_type=F32))

    share(0)
    for i in range(4):
        g_sum[i] = product(0, i)
    for i, part in enumerate(chunks):
        if i == 1:
            share(1)
        gh = product(1, i) + g_sum[i]
        for r in range(4):
            rs_out[part, r, 0:SUB] = gh[r * SUB:(r + 1) * SUB].astype(BF16)
            rs_out[part, r, SUB:PAD] = jnp.zeros((PAD - SUB, width), BF16)
        r_copies.append([send(rs_out.at[part, (x + dx) % 4], rs_in.at[x, part], r_sem, (i, dx),
                              at((x + dx) % 4, y, z, c)) for dx in (1, 2, 3)])

    for core in range(2):
        for h in range(2):
            low = core * HALF + h * PART
            gw[:, low:low + PART] = lax.dot_general(
                hid_t[...], rows[h, core].reshape(4 * CHUNK, PART), (((0,), (0,)), ((), ())),
                preferred_element_type=F32).astype(BF16)

    for i, part in enumerate(chunks):
        for copy in r_copies[i]:
            copy.wait_recv()
        gh = rs_out[part, x].astype(F32)[0:SUB]
        for dx in (1, 2, 3):
            gh = gh + rs_in[(x + dx) % 4, part].astype(F32)[0:SUB]
        dpre[0, part] = (gh * coef_g[part]).astype(BF16)
        dpre[1, part] = (gh * coef_u[part]).astype(BF16)

    sent = x_copies + h_copies
    for group in (a_copies, b_copies, y_copies, d_copies):
        sent += group.values()
    for group in r_copies:
        sent += group
    for copy in sent:
        copy.wait_send()


def per_device(grad_out, route_ids, route_probs, gate_up, w_down):
    width = gate_up.shape[5]
    vmem = pl.BlockSpec(memory_space=pltpu.VMEM)
    dma = pltpu.SemaphoreType.DMA
    dpre, gw = pl.pallas_call(
        kernel,
        out_shape=(
            jax.ShapeDtypeStruct((2, 4, SUB, width), BF16),
            jax.ShapeDtypeStruct((width, 2 * HALF), BF16),
        ),
        in_specs=[vmem, vmem, vmem, vmem, pl.BlockSpec(memory_space=pl.ANY)],
        out_specs=(vmem, vmem),
        scratch_shapes=[
            pltpu.VMEM((8, 2, WIDE), BF16),
            pltpu.VMEM((8, 2, WIDE), BF16),
            pltpu.VMEM((8, 4, 16, FIRST), BF16),
            pltpu.VMEM((8, 4, 16, PART), BF16),
            pltpu.VMEM((2, 3, CHUNK, PART), BF16),
            pltpu.VMEM((2, 2, 4, CHUNK, PART), BF16),
            pltpu.VMEM((width, 2 * HALF), BF16),
            pltpu.VMEM((512, 512), BF16),
            pltpu.VMEM((4, 4, PAD, width), BF16),
            pltpu.VMEM((4 * CHUNK, width), BF16),
            pltpu.VMEM((4, SUB, width), F32),
            pltpu.VMEM((4, SUB, width), F32),
            pltpu.VMEM((4, CHUNK, width), F32),
            pltpu.VMEM((4, 4, PAD, width), BF16),
            pltpu.VMEM((4, 4, PAD, width), BF16),
            dma(()),
            dma((2, 8)),
            dma((2, 4)),
            dma((2, 8)),
            dma((2, 64)),
            dma((2, 8)),
            dma((2, 8)),
            dma((2, 4, 4)),
        ],
        compiler_params=pltpu.CompilerParams(
            collective_id=0, has_side_effects=True, vmem_limit_bytes=60 * 1024 * 1024
        ),
    )(grad_out, route_ids, route_probs, gate_up.reshape(4, SUB, 2, width), w_down)
    grad_pre = jnp.moveaxis(dpre, 0, 2).reshape(gate_up.shape)
    return grad_pre, gw[None]


def solution(mesh):
    return jax.shard_map(
        per_device,
        mesh=mesh,
        in_specs=(
            P(("dp", "expert", "tensor"), None),
            P(("dp", "expert", "tensor"), None),
            P(("dp", "expert", "tensor"), None),
            P("dp", "expert", None, None, None, "tensor"),
            P("expert", "tensor", None),
        ),
        out_specs=(P("dp", "expert", None, None, None, "tensor"), P("expert", "tensor", "dp")),
        check_vma=False,
    )
```
